32 devices in a mesh: dp: 8 (over z, y), pipe: 4 (over x, core).
Axes of the slice: x: 2, y: 2, z: 4, core: 2. Of those that a mesh axis runs over, the one named last changes fastest.
Arguments:
- inputs: bfloat16 [32, 128, 768], P('dp', 'pipe'), may hold values from -6 to 6
- out_cotangent: bfloat16 [32, 128, 768], P('dp', 'pipe'), may hold values from -6 to 6
- positions: int32 [32, 128], P('dp'), may hold values from 0 to 381, as said below
- norm_gain: bfloat16 [8, 2, 768], P('pipe', None, 'dp'), may hold values from 0.25 to 1.75
- norm_bias: bfloat16 [8, 2, 768], P('pipe', None, 'dp'), may hold values from -1.796875 to 1.796875
- row_bias: bfloat16 [8, 3, 768], P('pipe', None, 'dp'), may hold values from -1.796875 to 1.796875
- w_query: bfloat16 [8, 768, 768], P('pipe', 'dp'), may hold values from -0.21875 to 0.21875
- w_keyval: bfloat16 [4, 768, 128], P('pipe', 'dp'), may hold values from -0.21875 to 0.21875
- keyval_bias: bfloat16 [4, 128], P('pipe', 'dp'), may hold values from -1.796875 to 1.796875
- w_output: bfloat16 [8, 768, 768], P('pipe', 'dp'), may hold values from -1.25 to 1.25
- w_up: bfloat16 [8, 768, 3072], P('pipe', 'dp'), may hold values from -0.21875 to 0.21875
- up_bias: bfloat16 [8, 3072], P('pipe', 'dp'), may hold values from -1.796875 to 1.796875
- w_down: bfloat16 [8, 3072, 768], P('pipe', 'dp'), may hold values from -0.109375 to 0.109375
Outputs:
- final: bfloat16 [32, 128, 768], P('dp', 'pipe')
- input_grad: bfloat16 [32, 128, 768], P('dp', 'pipe')
- grad_norm_gain: float32 [8, 2, 768], P('pipe', None, 'dp')
- grad_norm_bias: float32 [8, 2, 768], P('pipe', None, 'dp')
- grad_row_bias: float32 [8, 3, 768], P('pipe', None, 'dp')
- grad_query: float32 [8, 768, 768], P('pipe', 'dp')
- grad_keyval: float32 [4, 768, 128], P('pipe', 'dp')
- grad_keyval_bias: float32 [4, 128], P('pipe', 'dp')
- grad_output: float32 [8, 768, 768], P('pipe', 'dp')
- grad_up: float32 [8, 768, 3072], P('pipe', 'dp')
- grad_up_bias: float32 [8, 3072], P('pipe', 'dp')
- grad_down: float32 [8, 3072, 768], P('pipe', 'dp')
The draws below stay inside these ranges and needn't reach their ends.
Inputs may be any that keep to these rules, and one draw needn't show every extreme that they name: Each sequence's positions start at 0 and rise by 1 to 3 from one token to the next; in one sequence they rise by 3 at every step.
All inputs are finite; a program needn't handle non-finite values.
Results may differ from the reference program's by a relative error of at most 0.024.
Values may be sent and summed in bfloat16 or wider, within the bound.
No kernel may reach another device: no remote copies, remote signals or barrier semaphores. Data moves between devices by JAX's collectives and lax.ppermute only.
A program may use at most 256 MiB of HBM per device.

```python
import math
import jax
import jax.numpy as jnp
from jax import lax

D = 768
HEADS = 12
HEAD_DIM = 64
ROT_DIM = 16
FF = 3072
MICRO = 4
SEQ_LEN = 128
LAYERS = 8
SEQS = 32
N_PIPE = 4


def draw_positions(key, part):
    key = jax.random.fold_in(key, 7)
    spacing = jax.random.randint(key, (SEQS, SEQ_LEN), 1, 4)
    chosen = jax.random.randint(jax.random.fold_in(key, 11), (), 0, SEQS)
    column = lax.broadcasted_iota(jnp.int32, (SEQS, SEQ_LEN), 1)
    row = lax.broadcasted_iota(jnp.int32, (SEQS, SEQ_LEN), 0)
    spacing = jnp.where(row == chosen, 3, spacing)
    spacing = jnp.where(column == 0, 0, spacing)
    return jnp.cumsum(spacing, axis=1).astype(jnp.int32)


def spiked(values, stream_key, source, target, parts, factor):
    def block_of(axis_at):
        return (jnp.arange(values.shape[axis_at]) // (values.shape[axis_at] // parts)).reshape((-1,) + (1,) * (values.ndim - 1 - axis_at))

    first = jax.random.permutation(stream_key, parts)[block_of(target)]
    far = (block_of(target) + parts // 2) % parts
    return jnp.where((block_of(source) == first) | (block_of(source) == far), factor * values, values)


def steps_of(rng, shape, split, low, high):
    loudness, own = 1.0, jax.random.fold_in(rng, 6)
    for axis_at, blocks in split:
        heights = jnp.exp(jax.random.uniform(jax.random.fold_in(own, axis_at), (blocks,), jnp.float32, low / len(split), high / len(split)))
        loudness = loudness * jnp.repeat(heights, shape[axis_at] // blocks).reshape([-1 if axis == axis_at else 1 for axis in range(len(shape))])
    return loudness


def bell_draw(rng, dims, scale, most, pieces=(), held_as=jnp.bfloat16):
    gain = steps_of(rng, dims, pieces, -0.22, 0.18) if pieces else 1.0
    drawn = jax.random.normal(rng, dims, jnp.float32) * scale * gain
    return jnp.minimum(jnp.maximum(drawn, -most), most).astype(held_as)


def bell_draw_with(stream_key, extent, spread, reach, split, heavy, kind=jnp.bfloat16):
    entries = spread * jax.random.normal(stream_key, extent, jnp.float32)
    if split:
        entries = entries * steps_of(stream_key, extent, split, -0.22, 0.18)
    return jnp.clip(spiked(entries, jax.random.fold_in(stream_key, 3), *heavy), -reach, reach).astype(kind)


def setup_inputs(seed: int = 0) -> dict:
    key_of = jax.random.split(jax.random.key(seed), 14)
    inputs = bell_draw_with(key_of[0], (SEQS, SEQ_LEN, D), 1.0, 6.0, ((0, 8), (1, 4)), (0, 2, 8, 2.0))
    out_cotangent = bell_draw(key_of[1], (SEQS, SEQ_LEN, D), 1.0, 6.0, ((0, 8), (1, 4)))
    positions = draw_positions(jax.random.fold_in(key_of[13], 71), 0)
    norm_gain = jnp.clip(1.0 + 0.15 * jax.random.normal(key_of[3], (LAYERS, 2, D), jnp.float32), 0.25, 1.75).astype(jnp.bfloat16)
    norm_bias = bell_draw(key_of[4], (LAYERS, 2, D), 0.3, 1.796875, ((0, 4), (2, 8)))
    row_bias = bell_draw(key_of[5], (LAYERS, 3, D), 0.3, 1.796875, ((0, 4), (2, 8)))
    w_query = bell_draw(key_of[6], (LAYERS, D, D), D ** -0.5, 0.21875, ((0, 4), (1, 8)))
    w_keyval = bell_draw(key_of[7], (N_PIPE, D, 2 * HEAD_DIM), D ** -0.5, 0.21875, ((0, 4), (1, 8)))
    keyval_bias = bell_draw(key_of[8], (N_PIPE, 2 * HEAD_DIM), 0.3, 1.796875, ((0, 4), (1, 8)))
    w_output = bell_draw(key_of[9], (LAYERS, D, D), (D // 32) ** -0.5, 1.25, ((0, 4), (1, 8)))
    w_up = bell_draw(key_of[10], (LAYERS, D, FF), D ** -0.5, 0.21875, ((0, 4), (1, 8)))
    up_bias = bell_draw(key_of[11], (LAYERS, FF), 0.3, 1.796875, ((0, 4), (1, 8)))
    w_down = bell_draw(key_of[12], (LAYERS, FF, D), FF ** -0.5, 0.109375, ((0, 4), (1, 8)))
    return dict(inputs=inputs, out_cotangent=out_cotangent, positions=positions, norm_gain=norm_gain, norm_bias=norm_bias, row_bias=row_bias, w_query=w_query, w_keyval=w_keyval, keyval_bias=keyval_bias, w_output=w_output, w_up=w_up, up_bias=up_bias, w_down=w_down)


@jax.custom_vjp
def low(v):
    return lax.optimization_barrier(v.astype(jnp.bfloat16)).astype(jnp.float32)

@jax.custom_vjp
def low_back(v):
    return v

def low_keep(v):
    return (low(v), None)

def low_pass(kept, grad):
    return (grad,)

def back_keep(v):
    return (v, None)

def back_low(kept, grad):
    return (low(grad),)
low.defvjp(low_keep, low_pass)
low_back.defvjp(back_keep, back_low)
EPSILON = 1e-05
ROPE_BASE = 10000.0
POSITION_SCALE = 4.0
NEG_FILL = -1e+30

def layer_norm(values, norm_gain, norm_shift):
    average = lax.optimization_barrier(jnp.mean(values, axis=-1, keepdims=True))
    centered = values - average
    variance = lax.optimization_barrier(jnp.mean(centered * centered, axis=-1, keepdims=True))
    return centered * lax.rsqrt(variance + EPSILON) * norm_gain + norm_shift

def rope_tables(positions):
    half_width = ROT_DIM // 2
    inverse = ROPE_BASE ** (-2.0 * jnp.arange(half_width, dtype=jnp.float32) / ROT_DIM)
    angles = (positions.astype(jnp.float32) / POSITION_SCALE)[..., None] * inverse
    return (jnp.cos(angles), jnp.sin(angles))

def rotate(values, cosine, sine_part):
    half_width = ROT_DIM // 2
    first_half = values[..., :half_width]
    second = values[..., half_width:ROT_DIM]
    return jnp.concatenate([first_half * cosine - second * sine_part, second * cosine + first_half * sine_part, values[..., ROT_DIM:]], axis=-1)

def project(values, weight):
    return jnp.einsum('bsd,df->bsf', values, weight, precision=lax.Precision.HIGHEST)

def ref_layer(residual, layer_at, section_at, params, cosine, sine_part, shared):
    norm_gain, norm_bias, row_bias, w_query, w_keyval, keyval_bias, w_output, w_up, up_bias, w_down = params
    batch_size = residual.shape[0]
    row_count = residual.shape[1]
    attn_in = low(layer_norm(residual, norm_gain[layer_at, 0], norm_bias[layer_at, 0]))
    mlp_in = low(layer_norm(residual, norm_gain[layer_at, 1], norm_bias[layer_at, 1]))
    q_lin = low_back(project(attn_in, w_query[layer_at]) + row_bias[layer_at, 0])
    q_rot = low(rotate(q_lin.reshape(batch_size, row_count, HEADS, HEAD_DIM), cosine[:, :, None, :], sine_part[:, :, None, :]))
    if shared is None:
        kv_lin = low_back(project(attn_in, w_keyval[section_at]) + keyval_bias[section_at])
        key_rot = low(rotate(kv_lin[..., :HEAD_DIM], cosine, sine_part))
        value_low = low(kv_lin[..., HEAD_DIM:])
        shared = (key_rot, value_low)
    scores = jnp.einsum('bshd,btd->bhst', q_rot, shared[0], precision=lax.Precision.HIGHEST)
    scores = low_back(scores * (1.0 / math.sqrt(HEAD_DIM)))
    causal = lax.broadcasted_iota(jnp.int32, (row_count, row_count), 0) >= lax.broadcasted_iota(jnp.int32, (row_count, row_count), 1)
    probs = low(jax.nn.softmax(jnp.where(causal, scores, NEG_FILL), axis=-1))
    mixed = jnp.einsum('bhst,btd->bshd', probs, shared[1], precision=lax.Precision.HIGHEST).reshape(batch_size, row_count, D)
    mixed = low(low_back(mixed))
    branch = low_back(project(mixed, w_output[layer_at]) + row_bias[layer_at, 1])
    pre_act = low_back(project(mlp_in, w_up[layer_at]) + up_bias[layer_at])
    act_low = low(jax.nn.gelu(pre_act, approximate=False))
    feed_out = low_back(project(act_low, w_down[layer_at]) + row_bias[layer_at, 2])
    return (residual + branch + feed_out, shared)

def forward_all(params, start_rows, cosine, sine_part):
    residual = start_rows
    for section_at in range(N_PIPE):
        residual = low_back(residual)
        shared = None
        for sublayer in range(2):
            residual, shared = ref_layer(residual, 2 * section_at + sublayer, section_at, params, cosine, sine_part, shared)
        residual = low(residual)
    return residual

def reference(inputs, out_cotangent, positions, norm_gain, norm_bias, row_bias, w_query, w_keyval, keyval_bias, w_output, w_up, up_bias, w_down):
    params = tuple((item.astype(jnp.float32) for item in (norm_gain, norm_bias, row_bias, w_query, w_keyval, keyval_bias, w_output, w_up, up_bias, w_down)))
    group_count = SEQS // MICRO
    input_groups = inputs.astype(jnp.float32).reshape(group_count, MICRO, SEQ_LEN, D)
    cot_groups = out_cotangent.astype(jnp.float32).reshape(group_count, MICRO, SEQ_LEN, D)
    pos_groups = positions.reshape(group_count, MICRO, SEQ_LEN)

    def one_group(totals, batch):
        start_rows, cot_rows, pos_rows = batch
        cosine, sine_part = rope_tables(pos_rows)

        def forward_fn(param_set, entering):
            return forward_all(param_set, entering, cosine, sine_part)
        result, pull_back = jax.vjp(forward_fn, params, start_rows)
        param_grads, input_grads = pull_back(cot_rows)
        totals = jax.tree.map(lambda left_val, right_val: left_val + right_val, totals, param_grads)
        return (totals, (result, input_grads))
    zero_sums = jax.tree.map(lambda item: jnp.zeros(item.shape, jnp.float32), params)
    sums, (results, input_grads) = lax.scan(one_group, zero_sums, (input_groups, cot_groups, pos_groups))
    final = results.reshape(SEQS, SEQ_LEN, D).astype(jnp.bfloat16)
    input_grad = input_grads.reshape(SEQS, SEQ_LEN, D).astype(jnp.bfloat16)
    return (final, input_grad, sums[0], sums[1], sums[2], sums[3], sums[4], sums[5], sums[6], sums[7], sums[8], sums[9])
```

```python
import math

import jax
import jax.numpy as jnp
from jax import lax
from jax.experimental import pallas as pl
from jax.experimental.pallas import tpu as pltpu
from jax.sharding import PartitionSpec as P

D = 768
HEADS = 12
HEAD_DIM = 64
ROT_DIM = 16
FF = 3072
PAIRS = HEADS // 2
LANES = 128
TILE = 256

EPSILON = 1e-05
ROPE_BASE = 10000.0
POSITION_SCALE = 4.0
NEG_FILL = -1e30
SCALE = 1.0 / math.sqrt(HEAD_DIM)
LOG2E = math.log2(math.e)
PRM_ROWS = 16
VMEM_BYTES = 30 * 1024 * 1024
Q_UNROLL, A_UNROLL, U_UNROLL, O_UNROLL, L_UNROLL = 3, 6, 12, 3, 1

F32 = jnp.float32
BF16 = jnp.bfloat16


def place_of(section):
    column, which = section // 2, section % 2
    return column, (which if column % 2 == 0 else 1 - which)


def send(value, rule):
    pipe_count, dp_count = lax.axis_size("pipe"), lax.axis_size("dp")
    half = dp_count // 2
    pairs = []
    for h in range(2):
        for r in range(half):
            for i in range(pipe_count // 2):
                for c in range(2):
                    target = rule(h, r, i, c)
                    if target is not None:
                        th, tr, ti, tc = target
                        pairs.append(
                            (
                                (h * half + r) * pipe_count + 2 * i + c,
                                (th * half + tr) * pipe_count + 2 * ti + tc,
                            )
                        )
    return lax.ppermute(value, ("dp", "pipe"), pairs)


def swap_core(h, r, i, c):
    return h, r, i, 1 - c


def swap_half(h, r, i, c):
    return 1 - h, r, i, c


def swap_bit(bit):
    return lambda h, r, i, c: (h, r ^ bit, i, c)


def to_stage(step, stage_count):
    def rule(h, r, i, c):
        for stage in range(stage_count):
            if place_of(stage) == (i, h) and 0 <= stage + step < stage_count:
                ti, th = place_of(stage + step)
                return th, r, ti, c
        return None

    return rule


def nn(left, right):
    return lax.dot_general(left, right, (((1,), (0,)), ((), ())), preferred_element_type=F32)


def nt(left, right):
    return lax.dot_general(left, right, (((1,), (1,)), ((), ())), preferred_element_type=F32)


def tn(left, right):
    return lax.dot_general(left, right, (((0,), (0,)), ((), ())), preferred_element_type=F32)


def spin(values, cos_t, low_t, high_t):
    return values * cos_t + pltpu.roll(values, LANES - 8, 1) * low_t + pltpu.roll(values, 8, 1) * high_t


def unspin(values, cos_t, low_t, high_t):
    return values * cos_t - pltpu.roll(values, LANES - 8, 1) * low_t - pltpu.roll(values, 8, 1) * high_t


def doubled_keys(kv_low):
    kv = kv_low.astype(F32)
    lane = lax.broadcasted_iota(jnp.int32, kv.shape, 1)
    other = pltpu.roll(kv, HEAD_DIM, 1)
    zero = jnp.zeros_like(kv)
    keys = jnp.concatenate(
        [jnp.where(lane < HEAD_DIM, kv, zero), jnp.where(lane < HEAD_DIM, zero, other)], axis=0
    ).astype(BF16)
    vals = jnp.concatenate(
        [jnp.where(lane < HEAD_DIM, other, zero), jnp.where(lane < HEAD_DIM, zero, kv)], axis=0
    ).astype(BF16)
    return keys, vals


def gelu_parts(values):
    size = jnp.abs(values)
    bell = jnp.exp2(values * values * (-0.5 * LOG2E))
    t = 1.0 / (1.0 + (0.3275911 / math.sqrt(2.0)) * size)
    poly = 0.5 * 1.061405429
    for coef in (-1.453152027, 1.421413741, -0.284496736, 0.254829592):
        poly = poly * t + 0.5 * coef
    tail = poly * t * bell
    share = jnp.where(values >= 0.0, 1.0 - tail, tail)
    return values * share, share + values * (bell * (1.0 / math.sqrt(2.0 * math.pi)))


def fetch(source, target, sem):
    pltpu.make_async_copy(source, target, sem).start()


def landed(target, sem):
    pltpu.make_async_copy(target, target, sem).wait()


def pack_kernel(*refs):
    wq, wo, wu, wd, kvw, gain, shift, bias, kv_bias, up_bias = refs[:10]
    out_a, out_b, part_a, part_b, small, in_sems, out_sem = refs[10:]
    width, wide = wq.shape[1], wd.shape[1]
    body_rows = width + wide
    for layer in range(2):
        at = layer * body_rows
        for k in range(FF // D):
            fetch(
                wu.at[layer, :, pl.ds(k * D, D)], part_b.at[pl.ds(at + k * width, width)], in_sems.at[2 * layer + 1]
            )
        fetch(wo.at[layer], part_b.at[pl.ds(at + wide, width)], in_sems.at[2 * layer + 1])
    for layer in range(2):
        at = layer * body_rows
        fetch(wd.at[layer], part_a.at[pl.ds(at, wide)], in_sems.at[2 * layer])
        fetch(wq.at[layer], part_a.at[pl.ds(at + wide, width)], in_sems.at[2 * layer])
    last = pl.ds(2 * body_rows, 16)
    for k in range(width // 16):
        fetch(kvw.at[0, pl.ds(16 * k, 16)], part_a.at[last, pl.ds(k * LANES, LANES)], in_sems.at[4])
    small[...] = jnp.zeros_like(small)
    row = 0
    for item in (gain, shift, bias):
        for layer in range(2):
            for k in range(item.shape[1]):
                small[row : row + 1, :width] = item[layer, k : k + 1, :].astype(F32)
                row += 1
    small[row : row + 1, : kv_bias.shape[1]] = kv_bias[...].astype(F32)
    for layer in range(2):
        small[row + 1 : row + 2, layer * wide : (layer + 1) * wide] = up_bias[layer : layer + 1, :].astype(F32)
    for layer in range(2):
        landed(part_b.at[pl.ds(layer * body_rows, body_rows)], in_sems.at[2 * layer + 1])
    part_b[last, :] = small[...].astype(BF16)
    fetch(part_b, out_b, out_sem.at[0])
    for layer in range(2):
        landed(part_a.at[pl.ds(layer * body_rows, body_rows)], in_sems.at[2 * layer])
    landed(part_a.at[last], in_sems.at[4])
    fetch(part_a, out_a, out_sem.at[1])
    landed(out_b, out_sem.at[0])
    landed(out_a, out_sem.at[1])


def pack(w_query, w_output, w_up, w_down, w_keyval, small_items):
    width, wide = w_query.shape[1], w_down.shape[1]
    rows = 2 * (width + wide) + 16
    shape = pltpu.HBM((rows, D), BF16)
    return pl.pallas_call(
        pack_kernel,
        out_shape=[shape, shape],
        in_specs=any_specs(5) + [pl.BlockSpec(memory_space=pltpu.VMEM)] * 5,
        out_specs=[pl.BlockSpec(memory_space=pltpu.HBM)] * 2,
        scratch_shapes=[pltpu.VMEM((rows, D), BF16)] * 2
        + [pltpu.VMEM((16, D), F32), pltpu.SemaphoreType.DMA((5,)), pltpu.SemaphoreType.DMA((2,))],
        compiler_params=pltpu.CompilerParams(vmem_limit_bytes=58 * 1024 * 1024),
        name="pack_shard",
    )(w_query, w_output, w_up, w_down, w_keyval, *small_items)


def gather_kernel(count, width, wide, *refs):
    half = count // 2
    pieces = count + 2
    sc, own, other = refs[0], refs[1 : 1 + pieces], refs[1 + pieces : 1 + 2 * pieces]
    wq, wo, wu, wd = refs[-5:-1]
    sems = refs[-1]

    def lay(first, second):
        for place in range(count):
            at = pl.multiple_of(sc[1 + place] * width, 16)
            wide_at = pl.multiple_of(sc[1 + place] * wide, 16)
            split = place % half == half - 1
            for layer in range(2):
                index = place + place // half + (layer if split else 0)
                part_a, part_b = first[index], second[index]
                start = 0 if split else layer * (width + wide)
                fetch(part_a.at[pl.ds(start, wide)], wd.at[layer, pl.ds(wide_at, wide)], sems.at[3])
                fetch(part_a.at[pl.ds(start + wide, width)], wq.at[layer, pl.ds(at, width)], sems.at[0])
                for k in range(FF // D):
                    fetch(
                        part_b.at[pl.ds(start + k * width, width)],
                        wu.at[layer, pl.ds(at, width), pl.ds(k * D, D)],
                        sems.at[2],
                    )
                fetch(part_b.at[pl.ds(start + wide, width)], wo.at[layer, pl.ds(at, width)], sems.at[1])

    pl.when(sc[0] == 1)(lambda: lay(own, other))
    pl.when(sc[0] == 0)(lambda: lay(other, own))
    for index, target in enumerate((wq, wo, wu, wd)):
        landed(target, sems.at[index])


def copy_kernel(*refs):
    sources, targets, sems = refs[:4], refs[-5:-1], refs[-1]
    for index, (source, target) in enumerate(zip(sources, targets)):
        fetch(source, target, sems.at[index])
    for index, target in enumerate(targets):
        landed(target, sems.at[index])


def resident(scalars, own, other, width, wide):
    if scalars is None:
        lead, sources, kernel = [], own, copy_kernel
    else:
        flat = lambda lines: [item for line in lines for item in line[:-1] + line[-1]]
        lead, sources = [scalars], flat(own) + flat(other)
        kernel = lambda *refs: gather_kernel(D // width, width, wide, *refs)
    return pl.pallas_call(
        kernel,
        out_shape=[pltpu.VMEM((2,) + shape, BF16) for shape in ((D, D), (D, D), (D, FF), (FF, D))],
        in_specs=[pl.BlockSpec(memory_space=pltpu.SMEM)] * len(lead) + any_specs(len(sources)),
        out_specs=[pl.BlockSpec(memory_space=pltpu.VMEM)] * 4,
        scratch_shapes=[pltpu.SemaphoreType.DMA((4,))],
        compiler_params=pltpu.CompilerParams(vmem_limit_bytes=1024 * 1024),
        name="gather_shards",
    )(*lead, *[pltpu.with_memory_space_constraint(item, pltpu.HBM) for item in sources])


def weight_grad_kernel(layer, count, *refs):
    sc = refs[0]
    inputs = refs[1:8]
    more = refs[8:10] if layer == 0 else ()
    place = 8 + len(more)
    kept, given = refs[place : place + count], refs[place + count : place + 2 * count]
    scratch = refs[place + 2 * count :]
    held, part_a, part_b = scratch[:7], scratch[7], scratch[8]
    extra = scratch[9 : 9 + len(more)]
    in_sem, out_sem = scratch[-2:]
    g, d, u, m, a, q, o = held
    for index, (source, target) in enumerate(zip(inputs, held)):
        fetch(source, target, in_sem.at[index])
    width, wide = D // count, FF // count
    rows = g.shape[0]
    if more:
        fetch(more[0], extra[0], in_sem.at[7])
        fetch(more[1], part_b.at[:, pl.ds(width + wide, 16)], in_sem.at[8])
    landed(g, in_sem.at[0])
    landed(d, in_sem.at[1])
    for shard in range(count):
        cols = slice(shard * wide, (shard + 1) * wide)
        part_a[shard, :wide, :] = tn(g[:, cols], d[...]).astype(BF16)
    landed(u, in_sem.at[2])
    landed(m, in_sem.at[3])
    for k in range(FF // D):
        block = tn(m[...], u[:, k * D : (k + 1) * D]).astype(BF16)
        for shard in range(count):
            part_b[shard, k * width : (k + 1) * width, :] = block[shard * width : (shard + 1) * width]
    landed(a, in_sem.at[4])
    landed(q, in_sem.at[5])
    block = tn(a[...], q[...]).astype(BF16)
    for shard in range(count):
        part_a[shard, wide : wide + width, :] = block[shard * width : (shard + 1) * width]
    landed(o, in_sem.at[6])
    block = tn(o[...], d[...]).astype(BF16)
    for shard in range(count):
        part_b[shard, wide : wide + width, :] = block[shard * width : (shard + 1) * width]
    if more:
        landed(extra[0], in_sem.at[7])
        block = tn(a[...], extra[0][...]).astype(BF16)
        for shard in range(count):
            for k in range(width // 16):
                start = shard * width + 16 * k
                part_a[shard, width + wide :, k * LANES : (k + 1) * LANES] = block[start : start + 16]
        landed(part_b.at[:, pl.ds(width + wide, 16)], in_sem.at[8])

    def leave(first, second):
        for j in range(count):
            fetch(first.at[sc[1 + j]], kept[j], out_sem.at[j])
            fetch(second.at[sc[1 + j]], given[j], out_sem.at[count + j])

    pl.when(sc[0] == 1)(lambda: leave(part_a, part_b))
    pl.when(sc[0] == 0)(lambda: leave(part_b, part_a))
    for j in range(count):
        landed(kept[j], out_sem.at[j])
        landed(given[j], out_sem.at[count + j])


def weight_grads(scalars, inputs, more, layer, count):
    rows = inputs[0].shape[0]
    part_rows = (D + FF) // count + (16 if more else 0)
    part = pltpu.HBM((part_rows, D), BF16)
    flops = 4 * rows * D * (D + FF)
    results = pl.pallas_call(
        lambda *refs: weight_grad_kernel(layer, count, *refs),
        out_shape=[part] * (2 * count),
        in_specs=[pl.BlockSpec(memory_space=pltpu.SMEM)] + any_specs(7 + len(more)),
        out_specs=[pl.BlockSpec(memory_space=pltpu.HBM)] * (2 * count),
        scratch_shapes=[pltpu.VMEM(item.shape, BF16) for item in inputs]
        + [pltpu.VMEM((count, part_rows, D), BF16)] * 2
        + [pltpu.VMEM(item.shape, BF16) for item in more[:1]]
        + [pltpu.SemaphoreType.DMA((9,)), pltpu.SemaphoreType.DMA((2 * count,))],
        compiler_params=pltpu.CompilerParams(vmem_limit_bytes=58 * 1024 * 1024),
        cost_estimate=pl.CostEstimate(flops=flops, bytes_accessed=22_000_000, transcendentals=0),
        name="weight_grads",
    )(scalars, *inputs, *more)
    return results[:count], results[count:]


FWD_STASH = ("a", "m", "o", "q", "n", "g", "w", "p", "r")


def span(index, size):
    return pl.ds(pl.multiple_of(index * size, size), size)


def loop(count, unroll, step):
    def body(index, carry):
        step(index)
        return carry

    lax.fori_loop(0, count, body, 0, unroll=unroll)


def forward_kernel(tick, micro_count, *refs):
    sc, prm_h, tab_h, kvw_h, fresh_h, inc_h, wq, wo, wu, wd = refs[:10]
    place = 10 if tick == 0 else 10 + 20
    y_h, ys_h = refs[place : place + 2]
    stash_h = refs[place + 2 : place + 21]
    (
        kvw, prm, tab, xin, yout, s_a, s_m, s_o, s_q, s_n, s_g, s_w, s_p, s_r, s_kv, s_x, s_keys, s_vals,
        in_sem, out_sem,
    ) = refs[place + 21 :]
    stage = sc[0]
    slot = tick - 2 * stage
    rows = xin.shape[0]

    @pl.when((slot >= 0) & (slot < micro_count))
    def work():
        @pl.when(stage == 0)
        def take_fresh():
            fetch(fresh_h.at[slot], xin, in_sem.at[0])

        @pl.when(stage != 0)
        def take_sent():
            fetch(inc_h, xin, in_sem.at[0])

        fetch(prm_h, prm, in_sem.at[1])
        fetch(tab_h.at[slot], tab, in_sem.at[2])
        fetch(kvw_h, kvw, in_sem.at[3])
        landed(xin, in_sem.at[0])
        landed(prm, in_sem.at[1])
        landed(tab, in_sem.at[2])
        landed(kvw, in_sem.at[3])
        s_x[...] = xin[...].astype(F32)
        sources = (s_a, s_m, s_o, s_q, s_n, s_g, s_w, s_p, s_r)

        def kept(layer, index):
            number = 9 * layer + index
            return pltpu.make_async_copy(
                sources[index].at[layer], stash_h[number].at[slot], out_sem.at[number]
            )

        def keep(layer, index):
            for fixed in range(2):
                pl.when(layer == fixed)(lambda: kept(fixed, index).start())

        def one_layer(layer):
            x = s_x[...]
            row_of = lambda number: prm[layer, number : number + 1, :]
            mean = jnp.mean(x, axis=1, keepdims=True)
            centred = x - mean
            rstd = lax.rsqrt(jnp.mean(centred * centred, axis=1, keepdims=True) + EPSILON)
            normed = centred * rstd
            s_n[layer] = normed.astype(BF16)
            s_r[layer] = jnp.broadcast_to(rstd, (rows, LANES))
            s_a[layer] = (normed * row_of(0) + row_of(2)).astype(BF16)
            s_m[layer] = (normed * row_of(1) + row_of(3)).astype(BF16)
            for index in (0, 1, 4, 8):
                keep(layer, index)

            def query_tile(n):
                cols = span(n, TILE)
                q_lin = nn(s_a[layer], wq[layer, :, cols]) + prm[layer, 4:5, cols]
                turned = [
                    spin(q_lin[:, k * LANES : (k + 1) * LANES], tab[0], tab[1], tab[2])
                    for k in range(TILE // LANES)
                ]
                s_q[layer, :, cols] = jnp.concatenate(turned, axis=1).astype(BF16)

            loop(D // TILE, Q_UNROLL, query_tile)
            keep(layer, 3)

            @pl.when(layer == 0)
            def make_keys():
                col = lax.broadcasted_iota(jnp.int32, (rows, LANES), 1)
                kv_lin = nn(s_a[0], kvw[...]) + prm[0, 10:11, :LANES]
                s_kv[...] = jnp.where(
                    col < HEAD_DIM, spin(kv_lin, tab[0], tab[1], tab[2]), kv_lin
                ).astype(BF16)
                pltpu.make_async_copy(s_kv, stash_h[18].at[slot], out_sem.at[18]).start()
                s_keys[...], s_vals[...] = doubled_keys(s_kv[...])

            def attend(pair):
                cols = span(pair, LANES)
                row = lax.broadcasted_iota(jnp.int32, (rows, LANES), 0)
                col = lax.broadcasted_iota(jnp.int32, (rows, LANES), 1)
                scores = nt(s_q[layer, :, cols], s_keys[...]) * (SCALE * LOG2E)
                halves = []
                for side in range(2):
                    one = scores[:, side * LANES : (side + 1) * LANES]
                    one = jnp.where(row >= col, one, NEG_FILL)
                    raised = jnp.exp2(one - jnp.max(one, axis=1, keepdims=True))
                    halves.append(raised * (1.0 / jnp.sum(raised, axis=1, keepdims=True)))
                probs = jnp.concatenate(halves, axis=1).astype(BF16)
                s_p[layer, span(pair, rows), :] = probs
                s_o[layer, :, cols] = nn(probs, s_vals[...]).astype(BF16)

            loop(PAIRS, A_UNROLL, attend)
            keep(layer, 2)
            keep(layer, 7)

            def up_tile(n):
                cols = span(n, TILE)
                bias = prm[layer, pl.ds(6 + n // (D // TILE), 1), span(n % (D // TILE), TILE)]
                pre = nn(s_m[layer], wu[layer, :, cols]) + bias
                act, slope = gelu_parts(pre)
                s_g[layer, :, cols] = act.astype(BF16)
                s_w[layer, :, cols] = slope.astype(BF16)

            loop(FF // TILE, U_UNROLL, up_tile)
            keep(layer, 5)
            keep(layer, 6)

            def out_tile(n):
                cols = span(n, TILE)
                s_x[:, cols] = (
                    s_x[:, cols]
                    + nn(s_o[layer], wo[layer, :, cols])
                    + nn(s_g[layer], wd[layer, :, cols])
                    + prm[layer, 5:6, cols]
                )

            loop(D // TILE, O_UNROLL, out_tile)

        loop(2, L_UNROLL, one_layer)
        yout[...] = s_x[...].astype(BF16)
        last = [
            pltpu.make_async_copy(yout, y_h, out_sem.at[19]),
            pltpu.make_async_copy(yout, ys_h.at[slot], out_sem.at[20]),
        ]
        for copy in last:
            copy.start()
        for layer in range(2):
            for index in range(9):
                kept(layer, index).wait()
        pltpu.make_async_copy(s_kv, stash_h[18].at[slot], out_sem.at[18]).wait()
        for copy in last:
            copy.wait()


def backward_kernel(tick, micro_count, stage_count, *refs):
    sc, prm_h, tab_h, kvw_h, cot_h, inc_h, wq, wo, wu, wd = refs[:10]
    place = 10
    stash_h = refs[place : place + 11]
    place += 11 if tick == 0 else 11 + 9
    x_h, xs_h = refs[place : place + 2]
    outs_h = refs[place + 2 : place + 10]
    (
        kvw, prm, tab, din, dout, t_q, t_n, t_w, t_p, t_r, t_kv,
        s_d, s_u, s_q, s_kv, s_sum, d_mix, d_a, d_m, s_y, s_keys, s_vals, s_dk, s_dv, s_dkv,
        in_sem, st_sem, out_sem,
    ) = refs[place + 10 :]
    stage = sc[0]
    slot = tick - 2 * (stage_count - 1 - stage)
    rows = din.shape[0]

    @pl.when((slot >= 0) & (slot < micro_count))
    def work():
        @pl.when(stage == stage_count - 1)
        def take_given():
            fetch(cot_h.at[slot], din, in_sem.at[0])

        @pl.when(stage != stage_count - 1)
        def take_sent():
            fetch(inc_h, din, in_sem.at[0])

        fetch(prm_h, prm, in_sem.at[1])
        fetch(tab_h.at[slot], tab, in_sem.at[2])
        fetch(kvw_h, kvw, in_sem.at[3])
        fetch(stash_h[10].at[slot], t_kv, in_sem.at[4])
        for layer in (1, 0):
            for index, target in ((2, t_w), (3, t_p), (0, t_q), (1, t_n), (4, t_r)):
                fetch(stash_h[5 * layer + index].at[slot], target.at[layer], st_sem.at[layer, index])
        landed(din, in_sem.at[0])
        landed(prm, in_sem.at[1])
        landed(tab, in_sem.at[2])
        landed(kvw, in_sem.at[3])
        landed(t_kv, in_sem.at[4])
        s_y[...] = din[...].astype(F32)
        s_keys[...], s_vals[...] = doubled_keys(t_kv[...])
        s_sum[...] = jnp.zeros_like(s_sum)
        s_dkv[...] = jnp.zeros_like(s_dkv)
        sources = (s_d, s_u, s_q)

        def kept(layer, index):
            number = 3 * layer + index
            return pltpu.make_async_copy(
                sources[index].at[layer], outs_h[number].at[slot], out_sem.at[number]
            )

        def keep(layer, index):
            for fixed in range(2):
                pl.when(layer == fixed)(lambda: kept(fixed, index).start())

        def one_layer(turn):
            layer = 1 - turn
            lane = lax.broadcasted_iota(jnp.int32, (rows, LANES), 1)
            s_d[layer] = s_y[...].astype(BF16)
            keep(layer, 0)
            s_sum[layer, 5:6, :] = jnp.sum(s_d[layer].astype(F32), axis=0, keepdims=True)
            landed(t_w.at[layer], st_sem.at[layer, 2])

            def act_tile(n):
                cols = span(n, TILE)
                d_act = nt(s_d[layer], wd[layer, cols, :])
                d_pre = (d_act * t_w[layer, :, cols].astype(F32)).astype(BF16)
                s_u[layer, :, cols] = d_pre
                s_sum[layer, pl.ds(6 + n // (D // TILE), 1), span(n % (D // TILE), TILE)] = jnp.sum(
                    d_pre.astype(F32), axis=0, keepdims=True
                )

            loop(FF // TILE, U_UNROLL, act_tile)
            keep(layer, 1)

            def mix_tile(n):
                cols = span(n, TILE)
                d_mix[:, cols] = nt(s_d[layer], wo[layer, cols, :]).astype(BF16)
                d_m[:, cols] = nt(s_u[layer], wu[layer, cols, :])

            loop(D // TILE, O_UNROLL, mix_tile)
            landed(t_p.at[layer], st_sem.at[layer, 3])
            landed(t_q.at[layer], st_sem.at[layer, 0])
            s_dv[...] = jnp.zeros_like(s_dv)
            s_dk[...] = jnp.zeros_like(s_dk)

            def attend(pair):
                cols = span(pair, LANES)
                probs_low = t_p[layer, span(pair, rows), :]
                probs = probs_low.astype(F32)
                d_one = d_mix[:, cols]
                d_probs = nt(d_one, s_vals[...])
                halves = []
                for side in range(2):
                    part = slice(side * LANES, (side + 1) * LANES)
                    weighed = d_probs[:, part] * probs[:, part]
                    dot_row = jnp.sum(weighed, axis=1, keepdims=True)
                    halves.append(weighed - probs[:, part] * dot_row)
                d_scores = jnp.concatenate(halves, axis=1).astype(BF16)
                d_q = unspin(nn(d_scores, s_keys[...]) * SCALE, tab[0], tab[1], tab[2])
                s_q[layer, :, cols] = d_q.astype(BF16)
                s_dv[...] += tn(probs_low, d_one)
                s_dk[...] += tn(d_scores, t_q[layer, :, cols])

            loop(PAIRS, A_UNROLL, attend)
            keep(layer, 2)
            s_sum[layer, 4:5, :] = jnp.sum(s_q[layer].astype(F32), axis=0, keepdims=True)
            s_dkv[...] += jnp.where(
                lane < HEAD_DIM,
                (s_dk[:rows, :] + pltpu.roll(s_dk[rows:, :], HEAD_DIM, 1)) * SCALE,
                pltpu.roll(s_dv[:rows, :], HEAD_DIM, 1) + s_dv[rows:, :],
            )

            def back_tile(n):
                cols = span(n, TILE)
                d_a[:, cols] = nt(s_q[layer], wq[layer, cols, :])

            loop(D // TILE, Q_UNROLL, back_tile)

            @pl.when(layer == 0)
            def through_keys():
                total = s_dkv[...]
                turned = jnp.where(lane < HEAD_DIM, unspin(total, tab[0], tab[1], tab[2]), total)
                s_kv[...] = turned.astype(BF16)
                pltpu.make_async_copy(s_kv, outs_h[6].at[slot], out_sem.at[6]).start()
                s_sum[0, 10:11, :LANES] = jnp.sum(s_kv[...].astype(F32), axis=0, keepdims=True)
                d_a[...] += nt(s_kv[...], kvw[...])

            landed(t_n.at[layer], st_sem.at[layer, 1])
            landed(t_r.at[layer], st_sem.at[layer, 4])
            normed = t_n[layer].astype(F32)
            da, dm = d_a[...], d_m[...]
            s_sum[layer, 0:1, :] = jnp.sum(da * normed, axis=0, keepdims=True)
            s_sum[layer, 1:2, :] = jnp.sum(dm * normed, axis=0, keepdims=True)
            s_sum[layer, 2:3, :] = jnp.sum(da, axis=0, keepdims=True)
            s_sum[layer, 3:4, :] = jnp.sum(dm, axis=0, keepdims=True)
            d_normed = da * prm[layer, 0:1, :] + dm * prm[layer, 1:2, :]
            mean_one = jnp.mean(d_normed, axis=1, keepdims=True)
            mean_two = jnp.mean(d_normed * normed, axis=1, keepdims=True)
            s_y[...] += t_r[layer, :, 0:1] * (d_normed - mean_one - normed * mean_two)

        loop(2, L_UNROLL, one_layer)
        dout[...] = s_y[...].astype(BF16)
        last = [
            pltpu.make_async_copy(s_sum, outs_h[7].at[slot], out_sem.at[7]),
            pltpu.make_async_copy(dout, x_h, out_sem.at[8]),
            pltpu.make_async_copy(dout, xs_h.at[slot], out_sem.at[9]),
        ]
        for copy in last:
            copy.start()
        for layer in range(2):
            for index in range(3):
                kept(layer, index).wait()
        pltpu.make_async_copy(s_kv, outs_h[6].at[slot], out_sem.at[6]).wait()
        for copy in last:
            copy.wait()


def any_specs(how_many):
    return [pl.BlockSpec(memory_space=pl.ANY)] * how_many


def in_vmem(values):
    return [pltpu.with_memory_space_constraint(value, pltpu.VMEM) for value in values]


def call_tick(kernel, name, operands, carried, weight_count, scratch, rows):
    shapes = [jax.ShapeDtypeStruct((rows, D), BF16)] + [
        jax.ShapeDtypeStruct(item.shape, item.dtype) for item in carried
    ]
    carried = [item for item in carried if not isinstance(item, jax.ShapeDtypeStruct)]
    first_carried = len(operands)
    operands = operands + carried
    vmem = [pl.BlockSpec(memory_space=pltpu.VMEM)] * weight_count
    return pl.pallas_call(
        kernel,
        out_shape=shapes,
        in_specs=[pl.BlockSpec(memory_space=pltpu.SMEM)]
        + any_specs(5)
        + vmem
        + any_specs(len(operands) - 6 - weight_count),
        out_specs=any_specs(len(shapes)),
        input_output_aliases={first_carried + k: 1 + k for k in range(len(carried))},
        scratch_shapes=scratch,
        compiler_params=pltpu.CompilerParams(vmem_limit_bytes=VMEM_BYTES),
        cost_estimate=pl.CostEstimate(
            flops=4 * rows * D * (D + FF) * 2, bytes_accessed=10_000_000, transcendentals=0
        ),
        name=name,
    )(*operands)


def shared_scratch(rows):
    return [
        pltpu.VMEM((D, LANES), BF16),
        pltpu.VMEM((2, PRM_ROWS, D), F32),
        pltpu.VMEM((3, rows, LANES), F32),
        pltpu.VMEM((rows, D), BF16),
        pltpu.VMEM((rows, D), BF16),
    ]


def forward_tick(tick, scalars, fixed, given, incoming, weights, ys, stash, rows):
    micro_count = ys.shape[0]
    scratch = shared_scratch(rows) + [
        *[pltpu.VMEM((2, rows, D), BF16) for _ in range(5)],
        pltpu.VMEM((2, rows, FF), BF16),
        pltpu.VMEM((2, rows, FF), BF16),
        pltpu.VMEM((2, PAIRS * rows, 2 * LANES), BF16),
        pltpu.VMEM((2, rows, LANES), F32),
        pltpu.VMEM((rows, LANES), BF16),
        pltpu.VMEM((rows, D), F32),
        pltpu.VMEM((2 * rows, LANES), BF16),
        pltpu.VMEM((2 * rows, LANES), BF16),
        pltpu.SemaphoreType.DMA((4,)),
        pltpu.SemaphoreType.DMA((21,)),
    ]
    results = call_tick(
        lambda *refs: forward_kernel(tick, micro_count, *refs),
        "forward_tick",
        [scalars, *fixed, given, incoming, *in_vmem(weights)],
        [ys, *stash],
        len(weights),
        scratch,
        rows,
    )
    return results[0], results[1], list(results[2:])


def backward_tick(tick, stage_count, scalars, fixed, given, incoming, weights, stash, xs, outs, rows):
    micro_count = xs.shape[0]
    scratch = shared_scratch(rows) + [
        pltpu.VMEM((2, rows, D), BF16),
        pltpu.VMEM((2, rows, D), BF16),
        pltpu.VMEM((2, rows, FF), BF16),
        pltpu.VMEM((2, PAIRS * rows, 2 * LANES), BF16),
        pltpu.VMEM((2, rows, LANES), F32),
        pltpu.VMEM((rows, LANES), BF16),
        pltpu.VMEM((2, rows, D), BF16),
        pltpu.VMEM((2, rows, FF), BF16),
        pltpu.VMEM((2, rows, D), BF16),
        pltpu.VMEM((rows, LANES), BF16),
        pltpu.VMEM((2, PRM_ROWS, D), F32),
        pltpu.VMEM((rows, D), BF16),
        pltpu.VMEM((rows, D), F32),
        pltpu.VMEM((rows, D), F32),
        pltpu.VMEM((rows, D), F32),
        pltpu.VMEM((2 * rows, LANES), BF16),
        pltpu.VMEM((2 * rows, LANES), BF16),
        pltpu.VMEM((2 * rows, LANES), F32),
        pltpu.VMEM((2 * rows, LANES), F32),
        pltpu.VMEM((rows, LANES), F32),
        pltpu.SemaphoreType.DMA((5,)),
        pltpu.SemaphoreType.DMA((2, 5)),
        pltpu.SemaphoreType.DMA((10,)),
    ]
    results = call_tick(
        lambda *refs: backward_kernel(tick, micro_count, stage_count, *refs),
        "backward_tick",
        [scalars, *fixed, given, incoming, *in_vmem(weights), *stash],
        [xs, *outs],
        len(weights),
        scratch,
        rows,
    )
    return results[0], results[1], list(results[2:])


def rotary_tables(positions):
    half_width = ROT_DIM // 2
    inverse = ROPE_BASE ** (-2.0 * jnp.arange(half_width, dtype=F32) / ROT_DIM)
    angles = (positions.astype(F32) / POSITION_SCALE)[..., None] * inverse
    cosine, sine = jnp.cos(angles), jnp.sin(angles)
    rest = jnp.ones(angles.shape[:-1] + (HEAD_DIM - ROT_DIM,), F32)
    blank = jnp.zeros_like(cosine)
    cos_t = jnp.concatenate([cosine, cosine, rest] * 2, axis=-1)
    low_t = jnp.concatenate([-sine, blank, 0.0 * rest] * 2, axis=-1)
    high_t = jnp.concatenate([blank, sine, 0.0 * rest] * 2, axis=-1)
    return jnp.stack([cos_t, low_t, high_t], axis=-3)


def after(values, done):
    kept, unused = lax.optimization_barrier((tuple(values), tuple(done)))
    return list(kept)


def spread(part_a, part_b, native, half, tail_rows, before, beside, use_tails, late):
    side = lambda value: send(value, swap_bit(1))
    up = lambda value: send(value, swap_bit(2))
    core = lambda value: send(value, swap_core)
    received = core(part_b)
    here, away = jnp.where(native, part_a, received), jnp.where(native, received, part_a)
    move = lambda value: send(value, swap_half)
    if half != 4:
        own, other = [], []
        for start in (here, move(away)):
            line = [start]
            for mask in range(1, half):
                bit = mask & -mask
                line.append(send(line[mask ^ bit], swap_bit(bit)))
            own.append(line)
            other.append([core(value) for value in line])
        tails = [[item[-tail_rows:] for line in lines for item in line] for lines in (own, other)]
        return own, other, use_tails(*tails), late([])

    here, away = after([here, away], before)
    m0, n1, n2 = move(away), side(here), up(here)
    c0 = core(here)
    m0, n1, n2, c0 = after([m0, n1, n2, c0], [m0, n1, n2, c0] + beside)
    cut = (m0.shape[0] - tail_rows) // 2
    m1, m2 = side(m0), up(m0)
    n3 = [up(n1[:cut]), side(n2[cut:])]
    far_tail = send(m0[-tail_rows:], swap_bit(3))
    c1, c2, k0 = (core(value) for value in (n1, n2, m0))
    m1, m2, c1, c2, k0, far_tail, *n3 = after(
        [m1, m2, c1, c2, k0, far_tail, *n3], [m1, m2, c1, c2, k0, far_tail, *n3]
    )
    m3 = [up(m1[:cut]), side(m2[cut:])]
    k1, k2, far_other = core(m1), core(m2), core(far_tail)
    c3 = [core(value) for value in n3]
    late_done = late([k1])
    tails = [
        [item[-tail_rows:] for item in (*line, far)]
        for line, far in (((here, n1, n2, n3[1], m0, m1, m2), far_tail), ((c0, c1, c2, c3[1], k0, k1, k2), far_other))
    ]
    made = use_tails(*tails)
    m3 = after(m3, [*m3, k1, k2, *c3, *made])
    k3 = [core(value) for value in m3]
    own = [[here, n1, n2, n3], [m0, m1, m2, m3]]
    other = [[c0, c1, c2, c3], [k0, k1, k2, k3]]
    return own, other, made, late_done


def add_low(left, right):
    return (left.astype(F32) + right.astype(F32)).astype(BF16)


def reduce_home(make_parts, native, half, ended):
    side = lambda value: send(value, swap_bit(1))
    up = lambda value: send(value, swap_bit(2))
    core = lambda value: send(value, swap_core)
    move = lambda value: send(value, swap_half)

    def chip_sums(parts):
        kept, given = parts
        received = [[core(value) for value in line] for line in reversed(given)][::-1]
        return [[add_low(x, y) for x, y in zip(*lines)] for lines in zip(kept, received)]

    def finish(kept, moved):
        first = jnp.where(native, kept, moved)
        return first, core(jnp.where(native, moved, kept))

    if half != 4:
        results = []
        for layer in range(2):
            sums = chip_sums(make_parts(layer, []))
            for kind in range(2):
                bit = half // 2
                while bit:
                    for mask in range(bit):
                        sums[kind][mask] = add_low(sums[kind][mask], send(sums[kind][mask + bit], swap_bit(bit)))
                    bit //= 2
            results.append(finish(sums[0][0], move(sums[1][0])))
        return results

    n1, m1 = chip_sums(make_parts(1, []))
    s1, s3 = side(m1[1]), side(m1[3])
    n0, m0 = chip_sums(make_parts(0, ended))
    t2, t3 = up(m0[2]), up(m0[3])
    m1_0, m1_2 = add_low(m1[0], s1), add_low(m1[2], s3)
    m0_0, m0_1 = add_low(m0[0], t2), add_low(m0[1], t3)
    m1_2, m0_1 = after([m1_2, m0_1], [s1, s3, t2, t3])
    s2, t1 = up(m1_2), side(m0_1)
    m1_0, m0_0, *late = after([add_low(m1_0, s2), add_low(m0_0, t1), n1[1], n1[3], n0[1], n0[3]], [s2, t1])
    moved1, moved0 = move(m1_0), move(m0_0)
    a1, a3, b1, b3 = (side(value) for value in late)
    n1_0, n1_2 = add_low(n1[0], a1), add_low(n1[2], a3)
    n0_0, n0_2 = add_low(n0[0], b1), add_low(n0[2], b3)
    n1_0 = add_low(n1_0, up(n1_2))
    n0_0 = add_low(n0_0, up(n0_2))
    return [finish(n0_0, moved0), finish(n1_0, moved1)]


def pad_rows(flat, unit):
    short = -flat.shape[-1] % unit
    return jnp.pad(flat, [(0, 0)] * (flat.ndim - 1) + [(0, short)])


def body(
    inputs,
    out_cotangent,
    positions,
    norm_gain,
    norm_bias,
    row_bias,
    w_query,
    w_keyval,
    keyval_bias,
    w_output,
    w_up,
    up_bias,
    w_down,
):
    stage_count = lax.axis_size("pipe")
    replicas = lax.axis_size("dp")
    half = replicas // 2
    pipe_at, dp_at = lax.axis_index("pipe"), lax.axis_index("dp")
    column, core = pipe_at // 2, pipe_at % 2
    upper, replica = dp_at // half, dp_at % half
    stage = 2 * column + jnp.where(column % 2 == 0, upper, 1 - upper)
    micro_count, row_part = inputs.shape[:2]
    rows = row_part * stage_count
    width = D // replicas
    wide = FF // replicas

    (first_i, first_h), (last_i, last_h) = place_of(0), place_of(stage_count - 1)
    turn = stage_count // 2

    def whole_rows(entering, ending):
        starts, ends = [None] * stage_count, [None] * stage_count
        for source in range(stage_count):
            opposite = (source + turn) % stage_count

            def rule(h, r, i, c):
                if 2 * i + c == source:
                    return first_h, r, first_i, h
                return (last_h, r, last_i, h) if 2 * i + c == opposite else None

            part = send(jnp.where(pipe_at == source, entering, ending), rule)
            starts[source], ends[opposite] = part, part
        return jnp.concatenate(starts, axis=1), jnp.concatenate(ends, axis=1)

    def home_rows(leaving, started):
        final, grad = None, None
        for target in range(stage_count):
            opposite = (target + turn) % stage_count

            def rule(h, r, i, c):
                if (i, h) == (last_i, last_h):
                    return c, r, target // 2, target % 2
                return (c, r, opposite // 2, opposite % 2) if (i, h) == (first_i, first_h) else None

            rows_of = lambda value, at: value[:, at * row_part : (at + 1) * row_part]
            value = jnp.where(stage == stage_count - 1, rows_of(leaving, target), rows_of(started, opposite))
            part = send(value, rule)
            final = part if final is None else jnp.where(pipe_at == target, part, final)
            grad = part if grad is None else jnp.where(pipe_at == opposite, part, grad)
        return final, grad

    other_positions = send(positions, swap_half)
    tables = rotary_tables(jnp.where(core == upper, positions, other_positions))

    native = (column % 2 == 0) == (core == upper)
    small_items = (norm_gain, norm_bias, row_bias, keyval_bias, up_bias)
    kernels = width % 16 == 0 and half == 4
    body_rows = wide + width
    flat_rows = lambda item: pad_rows(item.reshape(-1), 16 * D).reshape(-1, D)
    small_shapes = [item.shape for item in small_items]
    small_counts = [4, 4, 6, 1, 1]
    if kernels:
        part_a, part_b = pack(w_query, w_output, w_up, w_down, w_keyval, small_items)
    else:
        lines = [item.reshape(count, -1) for item, count in zip(small_items, small_counts)]
        small_rows = jnp.concatenate([jnp.pad(line, ((0, 0), (0, D - line.shape[1]))) for line in lines])
        lines_a, lines_b = [], []
        for layer in range(2):
            lines_a += [w_down[layer], w_query[layer]]
            lines_b += [w_up[layer, :, k * D : (k + 1) * D] for k in range(FF // D)] + [w_output[layer]]
        part_a = jnp.concatenate(lines_a + [flat_rows(w_keyval)])
        part_b = jnp.concatenate(lines_b + [small_rows])
    masks = jnp.arange(half, dtype=jnp.int32)
    places = jnp.stack([upper * half + (masks ^ replica), (1 - upper) * half + (masks ^ replica)]).astype(jnp.int32)
    order = places.reshape(-1)
    inverse = jnp.zeros((replicas,), jnp.int32).at[order].set(jnp.arange(replicas, dtype=jnp.int32))
    tail_rows = part_a.shape[0] - 2 * body_rows
    flag = native.astype(jnp.int32).reshape(1)


    def use_tails(own_tails, other_tails):
        own_tails, other_tails = jnp.stack(own_tails), jnp.stack(other_tails)
        in_order = lambda picked: jnp.take(picked, inverse, axis=0)
        kv_all = in_order(jnp.where(native, own_tails, other_tails))
        small_all = in_order(jnp.where(native, other_tails, own_tails))
        if kernels:
            kv_weight = kv_all.reshape(replicas, 16, width // 16, LANES).swapaxes(1, 2).reshape(D, LANES)
        else:
            kv_weight = kv_all.reshape(replicas, -1)[:, : w_keyval.size].reshape(D, LANES)
        cuts = []
        used = 0
        for shape, count in zip(small_shapes, small_counts):
            size = math.prod(shape) // count
            cuts.append(small_all[:, used : used + count, :size].reshape((replicas,) + shape))
            used += count
        gains, shifts, biases = (
            jnp.moveaxis(cut, 0, 2).reshape(cut.shape[1:3] + (D,)).astype(F32) for cut in cuts[:3]
        )
        kv_bias = cuts[3].reshape(LANES).astype(F32)
        up_rows = jnp.moveaxis(cuts[4], 0, 1).reshape(2, FF // D, D).astype(F32)
        kv_row = jnp.zeros((2, 1, D), F32).at[0, 0, :LANES].set(kv_bias)
        params = jnp.concatenate(
            [
                gains,
                shifts,
                biases[:, 0:1],
                biases[:, 1:2] + biases[:, 2:3],
                up_rows,
                kv_row,
                jnp.zeros((2, PRM_ROWS - 7 - FF // D, D), F32),
            ],
            axis=1,
        )
        return params, kv_weight

    late = lambda done: whole_rows(*after([inputs, out_cotangent], done))
    own, other, (params, kv_weight), (fresh, given) = spread(
        part_a, part_b, native, half, tail_rows, [other_positions], [tables], use_tails, late
    )
    in_order = lambda picked: jnp.take(picked, inverse, axis=0)
    if kernels:
        weights = resident(jnp.concatenate([flag, order]), own, other, width, wide)
    else:
        mine, theirs = jnp.stack(own[0] + own[1]), jnp.stack(other[0] + other[1])
        all_a, all_b = in_order(jnp.where(native, mine, theirs)), in_order(jnp.where(native, theirs, mine))
        by_layer = lambda item: item[:, : 2 * body_rows].reshape(replicas, 2, body_rows, D).swapaxes(0, 1)
        all_a, all_b = by_layer(all_a), by_layer(all_b)
        up_part = jnp.swapaxes(all_b[:, :, :wide].reshape(2, replicas, FF // D, width, D), 2, 3)
        sources = [
            all_a[:, :, wide:].reshape(2, D, D),
            all_b[:, :, wide:].reshape(2, D, D),
            up_part.reshape(2, D, FF),
            all_a[:, :, :wide].reshape(2, FF, D),
        ]
        weights = resident(None, sources, [], width, wide)

    fixed = (params, tables, kv_weight)
    blank = jnp.zeros((rows, D), BF16)
    scalars = stage.astype(jnp.int32).reshape(1)

    slots = lambda shape, dtype=BF16: jax.ShapeDtypeStruct((micro_count,) + shape, dtype)
    per_layer = [
        *[slots((rows, D)) for _ in range(5)],
        slots((rows, FF)),
        slots((rows, FF)),
        slots((PAIRS * rows, 2 * LANES)),
        slots((rows, LANES), F32),
    ]
    stash = per_layer + per_layer + [slots((rows, LANES))]
    ticks = micro_count + 2 * (stage_count - 1)

    leaving, incoming, finals = blank, blank, slots((rows, D))
    for tick in range(ticks):
        arriving = send(leaving, to_stage(1, stage_count)) if 0 < tick < ticks - 1 else blank
        leaving, finals, stash = forward_tick(
            tick, scalars, fixed, fresh, incoming, weights, finals, stash, rows
        )
        incoming = arriving
    names = {name: (stash[k], stash[9 + k]) for k, name in enumerate(FWD_STASH)}
    back_stash = [names[name][layer] for layer in range(2) for name in ("q", "n", "w", "p", "r")] + [stash[18]]
    outs = []
    for layer in range(2):
        outs += [slots((rows, D)), slots((rows, FF)), slots((rows, D))]
    outs += [slots((rows, LANES)), slots((2, PRM_ROWS, D), F32)]

    leaving, incoming, starts = blank, blank, slots((rows, D))
    for tick in range(ticks):
        arriving = send(leaving, to_stage(-1, stage_count)) if 0 < tick < ticks - 1 else blank
        leaving, starts, outs = backward_tick(
            tick, stage_count, scalars, fixed, given, incoming, weights, back_stash, starts, outs, rows
        )
        incoming = arriving
    final, input_grad = home_rows(finals, starts)

    flat = lambda item: item.reshape(-1, item.shape[-1])
    sums = jnp.sum(outs[7], axis=0)
    by_shard = lambda item: jnp.moveaxis(item.reshape(item.shape[:2] + (replicas, -1)), 2, 0)
    up_sums = by_shard(sums[:, 6 : 6 + FF // D].reshape(2, 1, FF))
    tail = [
        by_shard(sums[:, 0:2]),
        by_shard(sums[:, 2:4]),
        by_shard(jnp.stack([sums[:, 4], sums[:, 5], sums[:, 5]], axis=1)),
        sums[0, 10, :LANES].reshape(replicas, -1),
        up_sums,
    ]
    tail = [item.reshape(replicas, count, -1) for item, count in zip(tail, small_counts)]
    tail = jnp.concatenate([jnp.pad(item, ((0, 0), (0, 0), (0, D - item.shape[2]))) for item in tail], axis=1)
    tail = tail.astype(BF16)

    def make_parts(layer, done):
        (d_low, u_low, q_low), (a_low, m_low, o_low, g_low) = (
            outs[3 * layer : 3 * layer + 3],
            [names[name][layer] for name in "amog"],
        )
        inputs = [flat(item) for item in (g_low, d_low, u_low, m_low, a_low, q_low, o_low)]
        inputs = after(inputs, done) if done else inputs
        g_low, d_low, u_low, m_low, a_low, q_low, o_low = inputs
        if kernels:
            lead = jnp.concatenate([native.astype(jnp.int32).reshape(1), order])
            more = [flat(outs[6]), tail] if layer == 0 else []
            kept, given = weight_grads(lead, inputs, more, layer, replicas)
            return [kept[:half], kept[half:]], [given[:half], given[half:]]
        product = lambda left, right: tn(left, right).astype(BF16)
        part_a = [
            product(g_low, d_low).reshape(replicas, wide, D),
            product(a_low, q_low).reshape(replicas, width, D),
        ]
        up = product(m_low, u_low).reshape(replicas, width, FF // D, D)
        part_b = [
            jnp.moveaxis(up, 2, 1).reshape(replicas, wide, D),
            product(o_low, d_low).reshape(replicas, width, D),
        ]
        if layer == 0:
            kv_grad = product(a_low, flat(outs[6])).reshape(replicas, -1)
            part_a.append(pad_rows(kv_grad, 16 * D).reshape(replicas, -1, D))
            part_b.append(tail)
        both = jnp.stack([jnp.concatenate(part_a, axis=1), jnp.concatenate(part_b, axis=1)])

        def pick(which):
            return [
                [
                    lax.dynamic_slice(both, (which, places[kind, mask], 0, 0), (1, 1) + both.shape[2:])[0, 0]
                    for mask in range(half)
                ]
                for kind in range(2)
            ]

        mine = jnp.where(native, 0, 1)
        return pick(mine), pick(1 - mine)

    shares = reduce_home(make_parts, native, half, [final, input_grad])
    grad_down = jnp.stack([part_a[:wide] for part_a, part_b in shares]).astype(F32)
    grad_query = jnp.stack([part_a[wide:body_rows] for part_a, part_b in shares]).astype(F32)
    grad_up = jnp.stack(
        [jnp.moveaxis(part_b[:wide].reshape(FF // D, width, D), 0, 1).reshape(width, FF) for part_a, part_b in shares]
    ).astype(F32)
    grad_output = jnp.stack([part_b[wide:body_rows] for part_a, part_b in shares]).astype(F32)
    kv_rows = shares[0][0][body_rows:]
    if kernels:
        kv_rows = kv_rows.reshape(16, width // 16, LANES).swapaxes(0, 1)
    grad_keyval = kv_rows.reshape(-1)[: w_keyval.size].reshape(w_keyval.shape).astype(F32)
    tail = shares[0][1][body_rows:].astype(F32)
    small = []
    used = 0
    for shape, count in zip(small_shapes, small_counts):
        small.append(tail[used : used + count, : math.prod(shape) // count].reshape(shape))
        used += count
    return (
        final,
        input_grad,
        small[0],
        small[1],
        small[2],
        grad_query,
        grad_keyval,
        small[3],
        grad_output,
        grad_up,
        small[4],
        grad_down,
    )


def solution(mesh):
    return jax.shard_map(
        body,
        mesh=mesh,
        in_specs=(
            P("dp", "pipe", None),
            P("dp", "pipe", None),
            P("dp", None),
            P("pipe", None, "dp"),
            P("pipe", None, "dp"),
            P("pipe", None, "dp"),
            P("pipe", "dp", None),
            P("pipe", "dp", None),
            P("pipe", "dp"),
            P("pipe", "dp", None),
            P("pipe", "dp", None),
            P("pipe", "dp"),
            P("pipe", "dp", None),
        ),
        out_specs=(
            P("dp", "pipe", None),
            P("dp", "pipe", None),
            P("pipe", None, "dp"),
            P("pipe", None, "dp"),
            P("pipe", None, "dp"),
            P("pipe", "dp", None),
            P("pipe", "dp", None),
            P("pipe", "dp"),
            P("pipe", "dp", None),
            P("pipe", "dp", None),
            P("pipe", "dp"),
            P("pipe", "dp", None),
        ),
        check_vma=False,
    )
```
